256 devices in a mesh: pipe: 8 (over z), expert: 32 (over x, y, core).
Axes of the slice: x: 4, y: 4, z: 8, core: 2. Of those that a mesh axis runs over, the one named last changes fastest.
Arguments:
- up_prev: bfloat16 [8, 3072, 3584], P('pipe', 'expert'), may hold values from -60 to 60
- down_prev: bfloat16 [8, 3072, 3584], P('pipe', 'expert'), may hold values from -60 to 60
- enter_up: bfloat16 [3072, 3584], P('expert'), may hold values from -60 to 60
- enter_down: bfloat16 [3072, 3584], P('expert'), may hold values from -60 to 60
- norm_gain: float32 [8, 3584], P('pipe'), may hold values from 0.1 to 1.9
- router: bfloat16 [8, 3584, 8], P('pipe'), may hold values from -0.09375 to 0.09375
- w_gate: bfloat16 [8, 3584, 8192], P('pipe', None, 'expert'), may hold values from -0.09375 to 0.09375
- w_up: bfloat16 [8, 3584, 8192], P('pipe', None, 'expert'), may hold values from -0.09375 to 0.09375
- w_down: bfloat16 [8, 8192, 3584], P('pipe', 'expert'), may hold values from -0.1875 to 0.1875
- ids_up: int32 [8, 3072, 2], P('pipe', 'expert'), may hold values from 0 to 7, all different within a row; in each aligned block of 96 rows (0 to 95, 96 to 191, ..., all dimensions but the last counted through in order) at most 30 rows name the same one
- ids_down: int32 [8, 3072, 2], P('pipe', 'expert'), may hold values from 0 to 7, all different within a row; in each aligned block of 96 rows (0 to 95, 96 to 191, ..., all dimensions but the last counted through in order) at most 30 rows name the same one
Outputs:
- up_next: bfloat16 [8, 3072, 3584], P('pipe', 'expert')
- down_next: bfloat16 [8, 3072, 3584], P('pipe', 'expert')
The draws below stay inside these ranges and needn't reach their ends.
Inputs may be any that keep to these rules, and one draw needn't show every extreme that they name: `ids_up`: within the 96 tokens of one index of expert (aligned blocks of rows), no expert is named by more than 30 tokens, a bound that some block reaches; a token names 2 different experts. `ids_down`: within the 96 tokens of one index of expert (aligned blocks of rows), no expert is named by more than 30 tokens, a bound that some block reaches; a token names 2 different experts.
All inputs are finite; a program needn't handle non-finite values.
Results may differ from the reference program's by a relative error of at most 0.008.
Values may be sent and summed in bfloat16 or wider, within the bound.
No kernel may reach another device: no remote copies, remote signals or barrier semaphores. Data moves between devices by JAX's collectives and lax.ppermute only.
A program may use at most 128 MiB of HBM per device.

```python
import math
import jax
import jax.numpy as jnp
import numpy as np
from jax import lax

D = 3584
HID = 1024
EXPERTS = 8
TOPK = 2
TOK_DEV = 96
CAP = 30
TOKENS = 3072
SPLIT = 4
N_PIPE = 8
N_EXPERT = 32


def scale_field(key, base):
    row_key, col_key = jax.random.split(key)
    row_scale = jnp.exp(jax.random.uniform(row_key, base.shape[:-1] + (1,), jnp.float32, math.log(0.3), math.log(3.0)))
    col_scale = jnp.exp(jax.random.uniform(col_key, (base.shape[-1],), jnp.float32, math.log(0.4), math.log(2.5)))
    return base * row_scale * col_scale


def draw_up_prev(key, part):
    key = jax.random.fold_in(key, 11)
    shape = (N_PIPE, TOKENS, D)
    base = jnp.clip(jax.random.normal(key, shape, jnp.float32), -5.0, 5.0)
    return scale_field(jax.random.fold_in(key, 5), base).astype(jnp.bfloat16)


def draw_down_prev(key, part):
    key = jax.random.fold_in(key, 12)
    shape = (N_PIPE, TOKENS, D)
    base = jnp.clip(jax.random.normal(key, shape, jnp.float32), -5.0, 5.0)
    return scale_field(jax.random.fold_in(key, 5), base).astype(jnp.bfloat16)


def draw_enter_up(key, part):
    key = jax.random.fold_in(key, 13)
    shape = (TOKENS, D)
    base = jnp.clip(jax.random.normal(key, shape, jnp.float32), -5.0, 5.0)
    return scale_field(jax.random.fold_in(key, 5), base).astype(jnp.bfloat16)


def draw_enter_down(key, part):
    key = jax.random.fold_in(key, 14)
    shape = (TOKENS, D)
    base = jnp.clip(jax.random.normal(key, shape, jnp.float32), -5.0, 5.0)
    return scale_field(jax.random.fold_in(key, 5), base).astype(jnp.bfloat16)


def block_scale(stream_key, dims, shards, low, high):
    def one(dim, parts):
        draws = jax.random.uniform(jax.random.fold_in(jax.random.fold_in(stream_key, 6), dim), (parts,), jnp.float32, low / len(shards), high / len(shards))
        return jnp.repeat(jnp.exp(draws), dims[dim] // parts).reshape((-1,) + (1,) * (len(dims) - dim - 1))

    level = one(*shards[0])
    for cut in shards[1:]:
        level = level * one(*cut)
    return level


def routed_block(stream_key, own, number, rows, amount, top, bound, skew):
    ranking = jax.random.permutation(stream_key, amount)
    crowded, ordinary = load_shares(amount, rows * top, bound, skew, True), load_shares(amount, rows * top, bound, skew, False)
    places = jnp.arange(amount)

    def named(lengths, offset_by):
        used = int((lengths > 0).sum())
        fixed = max(1, used // 4)
        moved = fixed + (places - fixed + offset_by * (used - fixed)) % max(1, amount - fixed)
        return jnp.zeros((amount,), jnp.int32).at[ranking[jnp.where(places < fixed, places, moved)]].set(jnp.asarray(lengths, jnp.int32))

    lengths = jnp.where(number % 4 == 0, named(crowded, number // 4), named(ordinary, number - number // 4 - 1))
    mixed = jax.random.permutation(jax.random.fold_in(own, 3), amount)
    giver, sink = mixed[0:amount // 2 * 2:2], mixed[1:amount // 2 * 2:2]
    slack = jnp.minimum(lengths[giver] - 1, bound - lengths[sink]) // 2
    slack = jnp.where((giver == ranking[0]) | (sink == ranking[0]) | (lengths[sink] == 0), 0, jnp.maximum(slack, 0))
    moved = jax.random.randint(jax.random.fold_in(own, 4), (amount // 2,), 0, 1 << 20) % (slack + 1)
    lengths = lengths.at[giver].add(-moved).at[sink].add(moved)
    members = jnp.searchsorted(jnp.cumsum(lengths), jnp.arange(rows * top), side="right").astype(jnp.int32)
    listing = members.reshape(top, rows).T
    listing = listing[jax.random.permutation(jax.random.fold_in(own, 1), rows)]
    offset_by = jax.random.randint(jax.random.fold_in(own, 2), (rows, 1), 0, top)
    return jnp.take_along_axis(listing, (jnp.arange(top)[None, :] + offset_by) % top, axis=1)


def load_shares(number_of, total, most, lean, full):
    portions = [(1 << 20) // math.isqrt(rank ** lean) + 1 for rank in range(1, number_of + 1)]
    largest = most if full else min(most, max(-(-total // number_of), total * portions[0] // sum(portions)))
    least = 1 if total - largest >= number_of - 1 else 0
    counts, surplus = [largest] + [least] * (number_of - 1), total - largest - least * (number_of - 1)
    while surplus > 0:
        candidates = [i for i in range(1, number_of) if counts[i] < largest] or [i for i in range(1, number_of) if counts[i] < most]
        pool, remaining = sum([portions[i] for i in candidates]), surplus
        for i in candidates:
            more = min(most - counts[i], max(1, remaining * portions[i] // pool), surplus)
            counts[i] = counts[i] + more
            surplus = surplus - more
    return np.array(counts)


def noise(stream_key, shape, deviation, reach, cuts=(), kind=jnp.bfloat16):
    level = block_scale(stream_key, shape, cuts, -0.22, 0.18) if cuts else 1.0
    values = jax.random.normal(stream_key, shape, jnp.float32) * deviation * level
    return jnp.minimum(jnp.maximum(values, -reach), reach).astype(kind)


def setup_inputs(seed: int = 0) -> dict:
    key_of = jax.random.split(jax.random.key(seed), 12)
    up_prev = draw_up_prev(jax.random.fold_in(key_of[11], 71), 0)
    down_prev = draw_down_prev(jax.random.fold_in(key_of[11], 71), 0)
    enter_up = draw_enter_up(jax.random.fold_in(key_of[11], 71), 0)
    enter_down = draw_enter_down(jax.random.fold_in(key_of[11], 71), 0)
    norm_gain = jnp.clip(1.0 + 0.18 * jax.random.normal(key_of[4], (N_PIPE, D), jnp.float32), 0.1, 1.9)
    router = noise(key_of[5], (N_PIPE, D, EXPERTS), D ** -0.5, 0.09375, ((0, 8),))
    w_gate = noise(key_of[6], (N_PIPE, D, EXPERTS * HID), D ** -0.5, 0.09375, ((0, 8), (2, 32)))
    w_up = noise(key_of[7], (N_PIPE, D, EXPERTS * HID), D ** -0.5, 0.09375, ((0, 8), (2, 32)))
    w_down = noise(key_of[8], (N_PIPE, EXPERTS * HID, D), HID ** -0.5, 0.1875, ((0, 8), (1, 32)))
    ids_up_keys = jax.random.split(jax.random.fold_in(key_of[9], 1), N_PIPE * TOKENS // TOK_DEV)
    ids_up_turns = jax.random.permutation(jax.random.fold_in(key_of[9], 3), N_PIPE * TOKENS // TOK_DEV)
    ids_up = jax.vmap(lambda own, number: routed_block(jax.random.fold_in(key_of[9], 2), own, number, TOK_DEV, EXPERTS, TOPK, CAP, 2))(ids_up_keys, ids_up_turns).reshape((N_PIPE, TOKENS, TOPK))
    ids_down_keys = jax.random.split(jax.random.fold_in(key_of[10], 1), N_PIPE * TOKENS // TOK_DEV)
    ids_down_turns = jax.random.permutation(jax.random.fold_in(key_of[10], 3), N_PIPE * TOKENS // TOK_DEV)
    ids_down = jax.vmap(lambda own, number: routed_block(jax.random.fold_in(key_of[10], 2), own, number, TOK_DEV, EXPERTS, TOPK, CAP, 2))(ids_down_keys, ids_down_turns).reshape((N_PIPE, TOKENS, TOPK))
    return {"up_prev": up_prev, "down_prev": down_prev, "enter_up": enter_up, "enter_down": enter_down, "norm_gain": norm_gain, "router": router, "w_gate": w_gate, "w_up": w_up, "w_down": w_down, "ids_up": ids_up, "ids_down": ids_down}


def normalize(stream_in, gain):
    values = stream_in.astype(jnp.float32)
    square_mean = lax.optimization_barrier(jnp.mean(values * values, axis=-1, keepdims=True))
    return (values * lax.rsqrt(square_mean + 1e-06) * gain).astype(jnp.bfloat16)

def gate_weights(normed, router_mat, routes):
    logits = jnp.dot(normed, router_mat, preferred_element_type=jnp.float32)
    choose = (routes[:, :, None] == jnp.arange(EXPERTS, dtype=jnp.int32)).astype(jnp.float32)
    chosen = lax.optimization_barrier(jnp.sum(choose * logits[:, None, :], axis=-1))
    affinity = jax.nn.sigmoid(chosen)
    return 2.5 * affinity / lax.optimization_barrier(jnp.sum(affinity, axis=-1, keepdims=True))

def block_slots(routes):
    marks = (routes[:, :, None] == jnp.arange(EXPERTS, dtype=jnp.int32)).astype(jnp.int32)
    flat_marks = marks.reshape(-1, EXPERTS)
    before = jnp.cumsum(flat_marks, axis=0) - flat_marks
    return lax.optimization_barrier(jnp.sum(before * flat_marks, axis=-1)).reshape(routes.shape).astype(jnp.int32)

def expert_ref(rows_in, gate_mat, up_mat, down_mat):
    gate_val = jnp.dot(rows_in, gate_mat, preferred_element_type=jnp.float32)
    up_val = jnp.dot(rows_in, up_mat, preferred_element_type=jnp.float32)
    hidden = (jax.nn.silu(gate_val) * up_val).astype(jnp.bfloat16)
    count = rows_in.shape[0]
    grouped = hidden.reshape(count, SPLIT, HID // SPLIT).astype(jnp.float32)
    down_groups = down_mat.reshape(SPLIT, HID // SPLIT, D).astype(jnp.float32)
    partial_value = jnp.einsum('rsh,shd->srd', grouped, down_groups).astype(jnp.bfloat16)
    return lax.optimization_barrier(jnp.sum(partial_value.astype(jnp.float32), axis=0))

def moe_layer(stream_in, routes, gain, router_mat, gate_all, up_all, down_all):
    normed = normalize(stream_in, gain)
    weights = gate_weights(normed, router_mat, routes)
    blocks = routes.reshape(N_EXPERT, TOK_DEV, TOPK)
    slots = jax.vmap(block_slots)(blocks)
    anchor = jnp.arange(N_EXPERT, dtype=jnp.int32)[:, None, None]
    index = (blocks * (N_EXPERT * CAP) + anchor * CAP + slots).reshape(-1).astype(jnp.int32)
    buffer = jnp.zeros((EXPERTS * N_EXPERT * CAP, D), jnp.bfloat16)
    buffer = buffer.at[index].set(jnp.repeat(normed, TOPK, axis=0))
    buffer = buffer.reshape(EXPERTS, N_EXPERT * CAP, D)
    gate_each = gate_all.reshape(D, EXPERTS, HID).transpose(1, 0, 2)
    up_each = up_all.reshape(D, EXPERTS, HID).transpose(1, 0, 2)
    down_each = down_all.reshape(EXPERTS, HID, D)
    outputs = lax.map(lambda packed: expert_ref(*packed), (buffer, gate_each, up_each, down_each))
    picked = outputs.reshape(-1, D)[index].reshape(TOKENS, TOPK, D)
    mixture = lax.optimization_barrier(jnp.sum(weights[:, :, None] * picked, axis=1))
    return (stream_in.astype(jnp.float32) + mixture).astype(jnp.bfloat16)

def reference(up_prev, down_prev, enter_up, enter_down, norm_gain, router, w_gate, w_up, w_down, ids_up, ids_down):
    input_up = jnp.concatenate([enter_up[None], up_prev[:-1]], axis=0)
    input_down = jnp.concatenate([down_prev[1:], enter_down[None]], axis=0)

    def section_step(packed):
        upward, downward, routes_up, routes_down, gain, router_mat, gate_all, up_all, down_all = packed
        first = moe_layer(upward, routes_up, gain, router_mat, gate_all, up_all, down_all)
        second = moe_layer(downward, routes_down, gain, router_mat, gate_all, up_all, down_all)
        return (first, second)
    up_next, down_next = lax.map(section_step, (input_up, input_down, ids_up, ids_down, norm_gain, router, w_gate, w_up, w_down))
    return (up_next, down_next)
```

```python
import functools

import jax
import jax.numpy as jnp
from jax import lax
from jax.experimental import pallas as pl
from jax.experimental.pallas import tpu as pltpu
from jax.sharding import PartitionSpec as P

EXPERTS = 8
SLOTS = 32
SIDE = 4
GROUP = EXPERTS * SLOTS
CHUNK = 512
ROOM = 60 * 1024 * 1024
VMEM = pl.BlockSpec(memory_space=pltpu.VMEM)
ANY = pl.BlockSpec(memory_space=pl.ANY)


def place(x, y, core):
    return (x * SIDE + y) * 2 + core


def moved(value, xor_y, xor_core):
    pairs = [
        (place(x, y, c), place(x, y ^ xor_y, c ^ xor_core)) for x in range(SIDE) for y in range(SIDE) for c in range(2)
    ]
    return lax.ppermute(value, "expert", pairs)


ALL_CHIPS = [[place(x, y, c) for x in range(SIDE) for y in range(SIDE)] for c in range(2)]
HALF_CHIPS = [[place(x, y, c) for x in range(SIDE) for y in ys] for ys in ((0, 3), (1, 2)) for c in range(2)]


def all_to_all(value, groups):
    return lax.all_to_all(value, "expert", split_axis=0, concat_axis=0, tiled=True, axis_index_groups=groups)


def from_behind(value, axis, by):
    devices = lax.axis_size(axis)
    pairs = [(i, i + by) for i in range(devices) if 0 <= i + by < devices]
    return lax.ppermute(value, axis, pairs)


def mm(a, b, dims=((1,), (0,))):
    return lax.dot_general(a, b, (dims, ((), ())), preferred_element_type=jnp.float32)


def chunks_of(width):
    return [slice(at, min(at + CHUNK, width)) for at in range(0, width, CHUNK)]


def prepare_kernel(at_end, earlier, recv, enter, gain, router_t, ids, *rest):
    sent, stream, combine, normed = rest[earlier:]
    tokens, width = recv.shape
    edge = lax.axis_index("pipe") == (lax.axis_size("pipe") - 1 if at_end else 0)
    total = jnp.zeros((tokens, 1), jnp.float32)
    for cut in chunks_of(width):
        values = jnp.where(edge, enter[:, cut].astype(jnp.float32), recv[:, cut].astype(jnp.float32))
        stream[:, cut] = values.astype(jnp.bfloat16)
        total += jnp.sum(values * values, axis=-1, keepdims=True)
    scale = lax.rsqrt(total / width + 1e-06)
    logits = jnp.zeros((EXPERTS, tokens), jnp.float32)
    for cut in chunks_of(width):
        part = (stream[:, cut].astype(jnp.float32) * scale * gain[:, cut]).astype(jnp.bfloat16)
        normed[:, cut] = part
        logits += mm(router_t[:, cut], part, ((1,), (1,)))

    row = lax.broadcasted_iota(jnp.int32, (tokens, tokens), 0)
    col = lax.broadcasted_iota(jnp.int32, (tokens, tokens), 1)
    expert = lax.broadcasted_iota(jnp.int32, (EXPERTS, tokens), 0)
    picks = [ids[k : k + 1, :] == expert for k in range(2)]
    marks = jnp.where(picks[0] | picks[1], 1.0, 0.0).astype(jnp.bfloat16)
    at = (expert * SLOTS).astype(jnp.float32) + mm(marks, jnp.where(row < col, 1.0, 0.0).astype(jnp.bfloat16))
    affinity = [jax.nn.sigmoid(jnp.sum(jnp.where(pick, logits, 0.0), axis=0, keepdims=True)) for pick in picks]
    both = affinity[0] + affinity[1]
    slot = lax.broadcasted_iota(jnp.int32, (GROUP, tokens), 0)
    placing = jnp.zeros((GROUP, tokens), jnp.float32)
    weighted = jnp.zeros((GROUP, tokens), jnp.float32)
    for pick, share in zip(picks, affinity):
        where = jnp.sum(jnp.where(pick, at, 0.0), axis=0, keepdims=True).astype(jnp.int32)
        placing += jnp.where(slot == where, 1.0, 0.0)
        weighted += jnp.where(slot == where, 2.5 * share / both, 0.0)
    placing = placing.astype(jnp.bfloat16)
    for cut in chunks_of(width):
        rows = mm(placing, normed[:, cut]).astype(jnp.bfloat16)
        for i in range(EXPERTS):
            block = rows[i * SLOTS : (i + 1) * SLOTS]
            sent[2 * i, :, cut] = block
            sent[2 * i + 1, :, cut] = block
    padded = jnp.concatenate([weighted, jnp.zeros((GROUP, -tokens % 128), jnp.float32)], axis=1)
    combine[...] = padded.T[:tokens]


def prepare(at_end, recv, enter, gain, router_t, ids, earlier):
    tokens, width = recv.shape
    shape = jax.ShapeDtypeStruct
    return pl.pallas_call(
        functools.partial(prepare_kernel, at_end, len(earlier)),
        out_shape=[
            shape((2 * EXPERTS, SLOTS, width), jnp.bfloat16),
            shape((tokens, width), jnp.bfloat16),
            shape((tokens, GROUP), jnp.float32),
        ],
        in_specs=[VMEM] * 5 + [ANY] * len(earlier),
        out_specs=[VMEM] * 3,
        scratch_shapes=[pltpu.VMEM((tokens, width), jnp.bfloat16)],
        compiler_params=pltpu.CompilerParams(vmem_limit_bytes=ROOM),
        cost_estimate=pl.CostEstimate(flops=2 * GROUP * tokens * width, bytes_accessed=18 * tokens * width, transcendentals=0),
        name="prepare",
    )(recv, enter, gain, router_t, ids.T, *earlier)


def hidden_kernel(blocks, gate_a, gate_b, up_a, up_b, kept, sent, gate_sum, up_sum):
    step = pl.program_id(0)

    @pl.when(step == 0)
    def _():
        gate_sum[...] = jnp.zeros_like(gate_sum)
        up_sum[...] = jnp.zeros_like(up_sum)

    rows = jnp.concatenate([blocks[x * SIDE + y] for ys in ((0, 3), (1, 2)) for x in range(SIDE) for y in ys], axis=0)
    half = gate_a.shape[1]
    for total, mats in ((gate_sum, (gate_a, gate_b)), (up_sum, (up_a, up_b))):
        for i, mat in enumerate(mats):
            total[:, i * half : (i + 1) * half] += mm(rows, mat[...])

    @pl.when(step == pl.num_programs(0) - 1)
    def _():
        my_y = lax.rem(lax.div(lax.axis_index("expert"), 2), SIDE)
        outer = (my_y == 0) | (my_y == 3)
        first, second = (
            jax.nn.silu(gate_sum[at : at + GROUP]) * up_sum[at : at + GROUP] for at in (0, GROUP)
        )
        kept[...] = jnp.where(outer, first, second).astype(jnp.bfloat16)
        sent[...] = jnp.where(outer, second, first).astype(jnp.bfloat16)


def hidden(blocks, gate_a, gate_b, up_a, up_b):
    width, half = gate_a.shape
    deep = width // 2
    shape = jax.ShapeDtypeStruct((GROUP, 2 * half), jnp.bfloat16)
    return pl.pallas_call(
        hidden_kernel,
        grid=(width // deep,),
        out_shape=[shape, shape],
        in_specs=[pl.BlockSpec((*blocks.shape[:2], deep), lambda k: (0, 0, k))]
        + [pl.BlockSpec((deep, half), lambda k: (k, 0))] * 4,
        out_specs=[pl.BlockSpec((GROUP, 2 * half), lambda k: (0, 0))] * 2,
        scratch_shapes=[pltpu.VMEM((2 * GROUP, 2 * half), jnp.float32)] * 2,
        compiler_params=pltpu.CompilerParams(vmem_limit_bytes=ROOM),
        cost_estimate=pl.CostEstimate(flops=16 * GROUP * width * half, bytes_accessed=12 * width * half, transcendentals=0),
        name="hidden",
    )(blocks, gate_a, gate_b, up_a, up_b)


def down_kernel(own, other, *rest):
    mats, out = rest[:-1], rest[-1]
    units = jnp.concatenate([own[...], other[...]], axis=1)
    mat = jnp.concatenate([mat[...] for mat in mats], axis=0)
    rows = mm(units, mat).astype(jnp.bfloat16)
    for i in range(EXPERTS):
        out[i] = rows[i * SLOTS : (i + 1) * SLOTS]


def down(own, other, mats):
    half, width = mats[0].shape
    deep = CHUNK
    return pl.pallas_call(
        down_kernel,
        grid=(width // deep,),
        out_shape=jax.ShapeDtypeStruct((EXPERTS, SLOTS, width), jnp.bfloat16),
        in_specs=[pl.BlockSpec(own.shape, lambda k: (0, 0))] * 2 + [pl.BlockSpec((mat.shape[0], deep), lambda k: (0, k)) for mat in mats],
        out_specs=pl.BlockSpec((EXPERTS, SLOTS, deep), lambda k: (0, 0, k)),
        compiler_params=pltpu.CompilerParams(vmem_limit_bytes=ROOM),
        cost_estimate=pl.CostEstimate(flops=8 * GROUP * width * half, bytes_accessed=10 * width * half, transcendentals=0),
        name="down",
    )(own, other, *mats)


def finish_kernel(stream, combine, blocks, out):
    tokens = stream.shape[0]
    weights = combine[...]
    high = weights.astype(jnp.bfloat16)
    left = weights - high.astype(jnp.float32)
    middle = left.astype(jnp.bfloat16)
    low = (left - middle.astype(jnp.float32)).astype(jnp.bfloat16)
    terms = jnp.concatenate([high, middle, low], axis=0)
    rows = jnp.concatenate([blocks[i] for i in range(EXPERTS)], axis=0)
    sums = mm(terms, rows)
    mixture = sums[:tokens] + sums[tokens : 2 * tokens] + sums[2 * tokens :]
    out[...] = (stream[...].astype(jnp.float32) + mixture).astype(jnp.bfloat16)


def finish(stream, combine, blocks):
    tokens, width = stream.shape
    deep = 2 * CHUNK if width % (2 * CHUNK) == 0 else CHUNK
    return pl.pallas_call(
        finish_kernel,
        grid=(width // deep,),
        out_shape=jax.ShapeDtypeStruct((tokens, width), jnp.bfloat16),
        in_specs=[
            pl.BlockSpec((tokens, deep), lambda k: (0, k)),
            pl.BlockSpec((tokens, GROUP), lambda k: (0, 0)),
            pl.BlockSpec((EXPERTS, SLOTS, deep), lambda k: (0, 0, k)),
        ],
        out_specs=pl.BlockSpec((tokens, deep), lambda k: (0, k)),
        compiler_params=pltpu.CompilerParams(vmem_limit_bytes=ROOM),
        cost_estimate=pl.CostEstimate(flops=6 * GROUP * width * tokens, bytes_accessed=10 * tokens * width, transcendentals=0),
        name="finish",
    )(stream, combine, blocks)


def after(value, earlier):
    return pl.pallas_call(
        lambda value, earlier, out: None,
        out_shape=jax.ShapeDtypeStruct(value.shape, value.dtype),
        in_specs=[ANY, ANY],
        out_specs=ANY,
        input_output_aliases={0: 0},
        name="after",
    )(value, earlier)


def body(up_prev, down_prev, enter_up, enter_down, norm_gain, router, w_gate, w_up, w_down, ids_up, ids_down):
    from_below = from_behind(up_prev[0], "pipe", 1)
    from_above = from_behind(down_prev[0], "pipe", -1)
    gate_a, up_a, down_a = w_gate[0], w_up[0], w_down[0]
    gate_b, up_b = moved(gate_a, 0, 1), moved(up_a, 0, 1)
    router_t = router[0].T
    part = down_a.shape[0] // 2
    down_c, down_e = moved(down_a[:part], 1, 0), moved(down_a[part:], 1, 0)
    down_mats = (down_a, moved(down_a, 0, 1), down_c, down_e, moved(down_c, 0, 1), moved(down_e, 0, 1))
    first = prepare(False, from_below, enter_up, norm_gain, router_t, ids_up[0], (gate_b, up_b, down_c))
    second = prepare(True, from_above, enter_down, norm_gain, router_t, ids_down[0], (first[0],))
    rows_first = all_to_all(first[0], ALL_CHIPS)
    rows_second = all_to_all(after(second[0], rows_first), ALL_CHIPS)
    outs = []
    for rows, (_, stream, combine) in ((rows_first, first), (rows_second, second)):
        kept, given = hidden(rows, gate_a, gate_b, up_a, up_b)
        results = down(kept, moved(given, 1, 0), down_mats)
        outs.append(finish(stream, combine, all_to_all(results, HALF_CHIPS))[None])
    return tuple(outs)


def solution(mesh):
    in_specs = (
        P("pipe", "expert", None),
        P("pipe", "expert", None),
        P("expert", None),
        P("expert", None),
        P("pipe", None),
        P("pipe", None, None),
        P("pipe", None, "expert"),
        P("pipe", None, "expert"),
        P("pipe", "expert", None),
        P("pipe", "expert", None),
        P("pipe", "expert", None),
    )
    out_specs = (P("pipe", "expert", None), P("pipe", "expert", None))
    return jax.shard_map(body, mesh=mesh, in_specs=in_specs, out_specs=out_specs, check_vma=False)
```

```python
import functools

import jax
import jax.numpy as jnp
from jax import lax
from jax.experimental import pallas as pl
from jax.experimental.pallas import tpu as pltpu
from jax.sharding import PartitionSpec as P

EXPERTS = 8
SLOTS = 32
SIDE = 4
GROUP = EXPERTS * SLOTS
CHUNK = 512
ROOM = 60 * 1024 * 1024
VMEM = pl.BlockSpec(memory_space=pltpu.VMEM)
ANY = pl.BlockSpec(memory_space=pl.ANY)


def place(x, y, core):
    return (x * SIDE + y) * 2 + core


def moved(value, by_x, xor_y, xor_core=0):
    pairs = [
        (place(x, y, c), place((x + by_x) % SIDE, y ^ xor_y, c ^ xor_core))
        for x in range(SIDE)
        for y in range(SIDE)
        for c in range(2)
    ]
    return lax.ppermute(value, "expert", pairs)


BLOCKS = [(by_x, xor_y) for xor_y in (0, 3) for by_x in range(SIDE)]
ORDER = [1, 3, 4, 2, 5, 7, 6]
ORDER_BACK = [4, 5, 7, 3, 1, 2, 6]


def from_behind(value, axis, by):
    devices = lax.axis_size(axis)
    pairs = [(i, i + by) for i in range(devices) if 0 <= i + by < devices]
    return lax.ppermute(value, axis, pairs)


def mm(a, b, dims=((1,), (0,))):
    return lax.dot_general(a, b, (dims, ((), ())), preferred_element_type=jnp.float32)


def chunks_of(width):
    return [slice(at, min(at + CHUNK, width)) for at in range(0, width, CHUNK)]


def prepare_one(at_end, at_row, recv, enter, gain, router_t, ids, blocks, stream, combine, normed):
    tokens, width = recv.shape
    edge = lax.axis_index("pipe") == (lax.axis_size("pipe") - 1 if at_end else 0)
    total = jnp.zeros((tokens, 1), jnp.float32)
    for cut in chunks_of(width):
        values = jnp.where(edge, enter[:, cut].astype(jnp.float32), recv[:, cut].astype(jnp.float32))
        stream[:, cut] = values.astype(jnp.bfloat16)
        total += jnp.sum(values * values, axis=-1, keepdims=True)
    scale = lax.rsqrt(total / width + 1e-06)
    logits = jnp.zeros((EXPERTS, tokens), jnp.float32)
    for cut in chunks_of(width):
        part = (stream[:, cut].astype(jnp.float32) * scale * gain[:, cut]).astype(jnp.bfloat16)
        normed[:, cut] = part
        logits += mm(router_t[:, cut], part, ((1,), (1,)))

    row = lax.broadcasted_iota(jnp.int32, (tokens, tokens), 0)
    col = lax.broadcasted_iota(jnp.int32, (tokens, tokens), 1)
    expert = lax.broadcasted_iota(jnp.int32, (EXPERTS, tokens), 0)
    picks = [ids[k : k + 1, :] == expert for k in range(2)]
    marks = jnp.where(picks[0] | picks[1], 1.0, 0.0).astype(jnp.bfloat16)
    spot = lax.axis_index("expert")
    my_x, my_half = lax.div(spot, 2 * SIDE), lax.rem(lax.div(spot, 4), 2)
    step = lax.rem(lax.div(expert, 2) - my_x + SIDE, SIDE)
    block = (lax.rem(expert, 2) ^ my_half) * SIDE + step
    at = (block * SLOTS).astype(jnp.float32) + mm(marks, jnp.where(row < col, 1.0, 0.0).astype(jnp.bfloat16))
    affinity = [jax.nn.sigmoid(jnp.sum(jnp.where(pick, logits, 0.0), axis=0, keepdims=True)) for pick in picks]
    both = affinity[0] + affinity[1]
    slot = lax.broadcasted_iota(jnp.int32, (GROUP, tokens), 0)
    placing = jnp.zeros((GROUP, tokens), jnp.float32)
    weighted = jnp.zeros((GROUP, tokens), jnp.float32)
    for pick, share in zip(picks, affinity):
        where = jnp.sum(jnp.where(pick, at, 0.0), axis=0, keepdims=True).astype(jnp.int32)
        placing += jnp.where(slot == where, 1.0, 0.0)
        weighted += jnp.where(slot == where, 2.5 * share / both, 0.0)
    placing = placing.astype(jnp.bfloat16)
    for cut in chunks_of(width):
        rows = mm(placing, normed[:, cut]).astype(jnp.bfloat16)
        for i, out in enumerate(blocks):
            out[at_row : at_row + SLOTS, cut] = rows[i * SLOTS : (i + 1) * SLOTS]
    padded = jnp.concatenate([weighted, jnp.zeros((GROUP, -tokens % 128), jnp.float32)], axis=1)
    combine[...] = padded.T[:tokens]


def prepare_kernel(earlier, recv_up, recv_down, enter_up, enter_down, gain, router_t, ids_up, ids_down, *rest):
    rest = rest[earlier:]
    blocks, (stream_up, stream_down, combine_up, combine_down, normed) = rest[:EXPERTS], rest[EXPERTS:]
    prepare_one(False, 0, recv_up, enter_up, gain, router_t, ids_up, blocks, stream_up, combine_up, normed)
    prepare_one(True, SLOTS, recv_down, enter_down, gain, router_t, ids_down, blocks, stream_down, combine_down, normed)


def prepare(recv_up, recv_down, enter_up, enter_down, gain, router_t, ids_up, ids_down, earlier):
    tokens, width = recv_up.shape
    shape = jax.ShapeDtypeStruct
    out = pl.pallas_call(
        functools.partial(prepare_kernel, len(earlier)),
        out_shape=[shape((2 * SLOTS, width), jnp.bfloat16)] * EXPERTS
        + [shape((tokens, width), jnp.bfloat16)] * 2
        + [shape((tokens, GROUP), jnp.float32)] * 2,
        in_specs=[VMEM] * 8 + [ANY] * len(earlier),
        out_specs=[VMEM] * (EXPERTS + 4),
        scratch_shapes=[pltpu.VMEM((tokens, width), jnp.bfloat16)],
        compiler_params=pltpu.CompilerParams(vmem_limit_bytes=ROOM),
        cost_estimate=pl.CostEstimate(flops=4 * GROUP * tokens * width, bytes_accessed=24 * tokens * width, transcendentals=0),
        name="prepare",
    )(recv_up, recv_down, enter_up, enter_down, gain, router_t, ids_up.T, ids_down.T, *earlier)
    return out[:EXPERTS], out[EXPERTS : EXPERTS + 2], out[EXPERTS + 2 :]


def hidden_kernel(*refs):
    blocks, gates, ups = refs[:EXPERTS], refs[EXPERTS : EXPERTS + 4], refs[EXPERTS + 4 : EXPERTS + 8]
    units, gate_sum, up_sum = refs[EXPERTS + 8 :]
    step = pl.program_id(0)

    @pl.when(step == 0)
    def _():
        gate_sum[...] = jnp.zeros_like(gate_sum)
        up_sum[...] = jnp.zeros_like(up_sum)

    rows = jnp.concatenate([block[...] for block in blocks], axis=0)
    part = gates[0].shape[1]
    for total, mats in ((gate_sum, gates), (up_sum, ups)):
        for i, mat in enumerate(mats):
            total[:, i * part : (i + 1) * part] += mm(rows, mat[...])

    @pl.when(step == pl.num_programs(0) - 1)
    def _():
        units[...] = (jax.nn.silu(gate_sum[...]) * up_sum[...]).astype(jnp.bfloat16)


def hidden(blocks, gates, ups):
    width, part = gates[0].shape
    deep = width // 2
    rows = 2 * GROUP
    return pl.pallas_call(
        hidden_kernel,
        grid=(width // deep,),
        out_shape=jax.ShapeDtypeStruct((rows, 4 * part), jnp.bfloat16),
        in_specs=[pl.BlockSpec((2 * SLOTS, deep), lambda k: (0, k))] * EXPERTS
        + [pl.BlockSpec((deep, part), lambda k: (k, 0))] * 8,
        out_specs=pl.BlockSpec((rows, 4 * part), lambda k: (0, 0)),
        scratch_shapes=[pltpu.VMEM((rows, 4 * part), jnp.float32)] * 2,
        compiler_params=pltpu.CompilerParams(vmem_limit_bytes=ROOM),
        cost_estimate=pl.CostEstimate(flops=0, bytes_accessed=0, transcendentals=0),
        name="hidden",
    )(*blocks, *gates, *ups)


def down_kernel(units, mat_a, mat_b, mat_c, mat_d, *blocks):
    mat = jnp.concatenate([mat_a[...], mat_b[...], mat_c[...], mat_d[...]], axis=0)
    rows = mm(units[...], mat).astype(jnp.bfloat16)
    for i, out in enumerate(blocks):
        out[...] = rows[i * 2 * SLOTS : (i + 1) * 2 * SLOTS]


def down(units, whole, parts, side):
    part, width = parts[0].shape
    deep = width // 2
    return pl.pallas_call(
        down_kernel,
        grid=(2,),
        out_shape=[jax.ShapeDtypeStruct((2 * SLOTS, width), jnp.bfloat16)] * EXPERTS,
        in_specs=[pl.BlockSpec(units.shape, lambda k: (0, 0))]
        + [pl.BlockSpec((part, deep), lambda k: (0, 2 * side + k))] * 2
        + [pl.BlockSpec((part, deep), lambda k: (0, k))] * 2,
        out_specs=[pl.BlockSpec((2 * SLOTS, deep), lambda k: (0, k))] * EXPERTS,
        compiler_params=pltpu.CompilerParams(vmem_limit_bytes=ROOM),
        cost_estimate=pl.CostEstimate(flops=0, bytes_accessed=0, transcendentals=0),
        name="down",
    )(units, *whole, *parts)


def finish_kernel(earlier, *refs):
    streams, combines, blocks, outs = refs[:2], refs[2:4], refs[4 : 4 + EXPERTS], refs[4 + EXPERTS + earlier :]
    tokens = streams[0].shape[0]
    for i in range(2):
        weights = combines[i][...]
        high = weights.astype(jnp.bfloat16)
        left = weights - high.astype(jnp.float32)
        middle = left.astype(jnp.bfloat16)
        low = (left - middle.astype(jnp.float32)).astype(jnp.bfloat16)
        terms = jnp.concatenate([high, middle, low], axis=0)
        rows = jnp.concatenate([block[i * SLOTS : (i + 1) * SLOTS] for block in blocks], axis=0)
        sums = mm(terms, rows)
        mixture = sums[:tokens] + sums[tokens : 2 * tokens] + sums[2 * tokens :]
        outs[i][...] = (streams[i][...].astype(jnp.float32) + mixture).astype(jnp.bfloat16)


def finish(streams, combines, blocks, side, begun):
    tokens, width = streams[0].shape
    deep = width // 4
    steps = blocks[0].shape[1] // deep
    column = pl.BlockSpec((tokens, deep), lambda k: (0, steps * side + k))
    return pl.pallas_call(
        functools.partial(finish_kernel, len(begun)),
        grid=(steps,),
        out_shape=[jax.ShapeDtypeStruct((tokens, width), jnp.bfloat16)] * 2,
        in_specs=[column] * 2
        + [pl.BlockSpec((tokens, GROUP), lambda k: (0, 0))] * 2
        + [pl.BlockSpec((2 * SLOTS, deep), lambda k: (0, k))] * EXPERTS
        + [ANY] * len(begun),
        out_specs=[column] * 2,
        input_output_aliases={4 + EXPERTS + i: i for i in range(len(begun))},
        compiler_params=pltpu.CompilerParams(vmem_limit_bytes=ROOM),
        cost_estimate=pl.CostEstimate(flops=6 * GROUP * width * tokens, bytes_accessed=8 * tokens * width, transcendentals=0),
        name="finish",
    )(*streams, *combines, *blocks, *begun)


def after(value, earlier):
    return pl.pallas_call(
        lambda *refs: None,
        out_shape=jax.ShapeDtypeStruct(value.shape, value.dtype),
        in_specs=[ANY] * (1 + len(earlier)),
        out_specs=ANY,
        input_output_aliases={0: 0},
        cost_estimate=pl.CostEstimate(flops=0, bytes_accessed=0, transcendentals=0),
        name="after",
    )(value, *earlier)


def exchange(blocks, sign, order, depth):
    out = {0: blocks[0]}
    for k, i in enumerate(order):
        block = after(blocks[i], (out[order[k - depth]],)) if k >= depth else blocks[i]
        out[i] = moved(block, sign * BLOCKS[i][0], BLOCKS[i][1])
    return [out[i] for i in range(EXPERTS)]


def body(up_prev, down_prev, enter_up, enter_down, norm_gain, router, w_gate, w_up, w_down, ids_up, ids_down):
    from_below = from_behind(up_prev[0], "pipe", 1)
    from_above = from_behind(down_prev[0], "pipe", -1)

    def of_core(value):
        return moved(value, 0, 0, 1)

    def of_pair(value):
        return moved(value, 0, 1)

    gate, up, whole = w_gate[0], w_up[0], w_down[0]
    gate_core, up_core = of_core(gate), of_core(up)
    blocks, streams, combines = prepare(
        from_below, from_above, enter_up, enter_down, norm_gain, router[0].T, ids_up[0], ids_down[0], (gate_core, up_core)
    )
    gate_pair, up_pair = of_pair(gate), of_pair(up)
    rows = exchange(blocks, 1, ORDER, 3)
    half = whole.shape[1] // 2
    low_pair = of_pair(after(whole[:, :half], (rows[ORDER[2]],)))
    high_pair = of_pair(after(whole[:, half:], (rows[ORDER[5]],)))
    gate_pair, up_pair = after(gate_pair, rows[1:]), after(up_pair, rows[1:])
    units = hidden(rows, (gate, gate_core, gate_pair, of_core(gate_pair)), (up, up_core, up_pair, of_core(up_pair)))
    own = (whole, of_core(whole))
    low_pair = after(low_pair, (units,))
    back = exchange(down(units, own, (low_pair, of_core(low_pair)), 0), -1, ORDER_BACK, 5)
    high_pair = after(high_pair, [back[i] for i in ORDER_BACK[:3]])
    outs = finish(streams, combines, back, 0, ())
    back = exchange(down(units, own, (high_pair, of_core(high_pair)), 1), -1, ORDER_BACK, 5)
    outs = finish(streams, combines, back, 1, outs)
    return outs[0][None], outs[1][None]


def solution(mesh):
    in_specs = (
        P("pipe", "expert", None),
        P("pipe", "expert", None),
        P("expert", None),
        P("expert", None),
        P("pipe", None),
        P("pipe", None, None),
        P("pipe", None, "expert"),
        P("pipe", None, "expert"),
        P("pipe", "expert", None),
        P("pipe", "expert", None),
        P("pipe", "expert", None),
    )
    out_specs = (P("pipe", "expert", None), P("pipe", "expert", None))
    return jax.shard_map(body, mesh=mesh, in_specs=in_specs, out_specs=out_specs, check_vma=False)
```

```python
import functools

import jax
import jax.numpy as jnp
from jax import lax
from jax.experimental import pallas as pl
from jax.experimental.pallas import tpu as pltpu
from jax.sharding import PartitionSpec as P

EXPERTS = 8
SLOTS = 32
SIDE = 4
GROUP = EXPERTS * SLOTS
CHUNK = 512
ROOM = 60 * 1024 * 1024
VMEM = pl.BlockSpec(memory_space=pltpu.VMEM)
ANY = pl.BlockSpec(memory_space=pl.ANY)


def place(x, y, core):
    return (x * SIDE + y) * 2 + core


def moved(value, by_x, xor_y, xor_core=0):
    pairs = [
        (place(x, y, c), place((x + by_x) % SIDE, y ^ xor_y, c ^ xor_core))
        for x in range(SIDE)
        for y in range(SIDE)
        for c in range(2)
    ]
    return lax.ppermute(value, "expert", pairs)


BLOCKS = [(by_x, xor_y) for xor_y in (0, 3) for by_x in range(SIDE)]
ORDER = [1, 3, 4, 2, 5, 7, 6]
ORDER_LOW = [5, 7, 2, 4, 1, 3, 6]
ORDER_HIGH = [6, 2, 5, 7, 1, 3, 4]


def from_behind(value, axis, by):
    devices = lax.axis_size(axis)
    pairs = [(i, i + by) for i in range(devices) if 0 <= i + by < devices]
    return lax.ppermute(value, axis, pairs)


def mm(a, b, dims=((1,), (0,))):
    return lax.dot_general(a, b, (dims, ((), ())), preferred_element_type=jnp.float32)


def chunks_of(width):
    return [slice(at, min(at + CHUNK, width)) for at in range(0, width, CHUNK)]


def prepare_one(at_end, at_row, recv, enter, gain, router_t, ids, blocks, stream, combine, normed):
    tokens, width = recv.shape
    edge = lax.axis_index("pipe") == (lax.axis_size("pipe") - 1 if at_end else 0)
    total = jnp.zeros((tokens, 1), jnp.float32)
    for cut in chunks_of(width):
        values = jnp.where(edge, enter[:, cut].astype(jnp.float32), recv[:, cut].astype(jnp.float32))
        stream[:, cut] = values.astype(jnp.bfloat16)
        total += jnp.sum(values * values, axis=-1, keepdims=True)
    scale = lax.rsqrt(total / width + 1e-06)
    logits = jnp.zeros((EXPERTS, tokens), jnp.float32)
    for cut in chunks_of(width):
        part = (stream[:, cut].astype(jnp.float32) * scale * gain[:, cut]).astype(jnp.bfloat16)
        normed[:, cut] = part
        logits += mm(router_t[:, cut], part, ((1,), (1,)))

    row = lax.broadcasted_iota(jnp.int32, (tokens, tokens), 0)
    col = lax.broadcasted_iota(jnp.int32, (tokens, tokens), 1)
    expert = lax.broadcasted_iota(jnp.int32, (EXPERTS, tokens), 0)
    picks = [ids[k : k + 1, :] == expert for k in range(2)]
    marks = jnp.where(picks[0] | picks[1], 1.0, 0.0).astype(jnp.bfloat16)
    spot = lax.axis_index("expert")
    my_x, my_half = lax.div(spot, 2 * SIDE), lax.rem(lax.div(spot, 4), 2)
    step = lax.rem(lax.div(expert, 2) - my_x + SIDE, SIDE)
    block = (lax.rem(expert, 2) ^ my_half) * SIDE + step
    at = (block * SLOTS).astype(jnp.float32) + mm(marks, jnp.where(row < col, 1.0, 0.0).astype(jnp.bfloat16))
    affinity = [jax.nn.sigmoid(jnp.sum(jnp.where(pick, logits, 0.0), axis=0, keepdims=True)) for pick in picks]
    both = affinity[0] + affinity[1]
    slot = lax.broadcasted_iota(jnp.int32, (GROUP, tokens), 0)
    placing = jnp.zeros((GROUP, tokens), jnp.float32)
    weighted = jnp.zeros((GROUP, tokens), jnp.float32)
    for pick, share in zip(picks, affinity):
        where = jnp.sum(jnp.where(pick, at, 0.0), axis=0, keepdims=True).astype(jnp.int32)
        placing += jnp.where(slot == where, 1.0, 0.0)
        weighted += jnp.where(slot == where, 2.5 * share / both, 0.0)
    placing = placing.astype(jnp.bfloat16)
    for cut in chunks_of(width):
        rows = mm(placing, normed[:, cut]).astype(jnp.bfloat16)
        for i, out in enumerate(blocks):
            out[at_row : at_row + SLOTS, cut] = rows[i * SLOTS : (i + 1) * SLOTS]
    padded = jnp.concatenate([weighted, jnp.zeros((GROUP, -tokens % 128), jnp.float32)], axis=1)
    combine[...] = padded.T[:tokens]


def prepare_kernel(earlier, recv_up, recv_down, enter_up, enter_down, gain, router_t, ids_up, ids_down, *rest):
    rest = rest[earlier:]
    blocks, (stream_up, stream_down, combine_up, combine_down, normed) = rest[:EXPERTS], rest[EXPERTS:]
    prepare_one(False, 0, recv_up, enter_up, gain, router_t, ids_up, blocks, stream_up, combine_up, normed)
    prepare_one(True, SLOTS, recv_down, enter_down, gain, router_t, ids_down, blocks, stream_down, combine_down, normed)


def prepare(recv_up, recv_down, enter_up, enter_down, gain, router_t, ids_up, ids_down, earlier):
    tokens, width = recv_up.shape
    shape = jax.ShapeDtypeStruct
    out = pl.pallas_call(
        functools.partial(prepare_kernel, len(earlier)),
        out_shape=[shape((2 * SLOTS, width), jnp.bfloat16)] * EXPERTS
        + [shape((tokens, width), jnp.bfloat16)] * 2
        + [shape((tokens, GROUP), jnp.float32)] * 2,
        in_specs=[VMEM] * 8 + [ANY] * len(earlier),
        out_specs=[VMEM] * (EXPERTS + 4),
        scratch_shapes=[pltpu.VMEM((tokens, width), jnp.bfloat16)],
        compiler_params=pltpu.CompilerParams(vmem_limit_bytes=ROOM),
        cost_estimate=pl.CostEstimate(flops=4 * GROUP * tokens * width, bytes_accessed=24 * tokens * width, transcendentals=0),
        name="prepare",
    )(recv_up, recv_down, enter_up, enter_down, gain, router_t, ids_up.T, ids_down.T, *earlier)
    return out[:EXPERTS], out[EXPERTS : EXPERTS + 2], out[EXPERTS + 2 :]


def hidden_kernel(*refs):
    blocks, gates, ups = refs[:EXPERTS], refs[EXPERTS : EXPERTS + 4], refs[EXPERTS + 4 : EXPERTS + 8]
    units, gate_sum, up_sum = refs[EXPERTS + 8 :]
    step = pl.program_id(0)

    @pl.when(step == 0)
    def _():
        gate_sum[...] = jnp.zeros_like(gate_sum)
        up_sum[...] = jnp.zeros_like(up_sum)

    rows = jnp.concatenate([block[...] for block in blocks], axis=0)
    part = gates[0].shape[1]
    for total, mats in ((gate_sum, gates), (up_sum, ups)):
        for i, mat in enumerate(mats):
            total[:, i * part : (i + 1) * part] += mm(rows, mat[...])

    @pl.when(step == pl.num_programs(0) - 1)
    def _():
        units[...] = (jax.nn.silu(gate_sum[...]) * up_sum[...]).astype(jnp.bfloat16)


def hidden(blocks, gates, ups):
    width, part = gates[0].shape
    deep = width // 2
    rows = 2 * GROUP
    return pl.pallas_call(
        hidden_kernel,
        grid=(width // deep,),
        out_shape=jax.ShapeDtypeStruct((rows, 4 * part), jnp.bfloat16),
        in_specs=[pl.BlockSpec((2 * SLOTS, deep), lambda k: (0, k))] * EXPERTS
        + [pl.BlockSpec((deep, part), lambda k: (k, 0))] * 8,
        out_specs=pl.BlockSpec((rows, 4 * part), lambda k: (0, 0)),
        scratch_shapes=[pltpu.VMEM((rows, 4 * part), jnp.float32)] * 2,
        compiler_params=pltpu.CompilerParams(vmem_limit_bytes=ROOM),
        cost_estimate=pl.CostEstimate(flops=0, bytes_accessed=0, transcendentals=0),
        name="hidden",
    )(*blocks, *gates, *ups)


def down_kernel(units, mat_a, mat_b, mat_c, mat_d, *blocks):
    mat = jnp.concatenate([mat_a[...], mat_b[...], mat_c[...], mat_d[...]], axis=0)
    rows = mm(units[...], mat).astype(jnp.bfloat16)
    for i, out in enumerate(blocks):
        out[...] = rows[i * 2 * SLOTS : (i + 1) * 2 * SLOTS]


def down(units, whole, parts, side):
    part, width = parts[0].shape
    deep = width // 2
    return pl.pallas_call(
        down_kernel,
        grid=(2,),
        out_shape=[jax.ShapeDtypeStruct((2 * SLOTS, width), jnp.bfloat16)] * EXPERTS,
        in_specs=[pl.BlockSpec(units.shape, lambda k: (0, 0))]
        + [pl.BlockSpec((part, deep), lambda k: (0, 2 * side + k))] * 2
        + [pl.BlockSpec((part, deep), lambda k: (0, k))] * 2,
        out_specs=[pl.BlockSpec((2 * SLOTS, deep), lambda k: (0, k))] * EXPERTS,
        compiler_params=pltpu.CompilerParams(vmem_limit_bytes=ROOM),
        cost_estimate=pl.CostEstimate(flops=0, bytes_accessed=0, transcendentals=0),
        name="down",
    )(units, *whole, *parts)


def finish_kernel(earlier, *refs):
    streams, combines, blocks, outs = refs[:2], refs[2:4], refs[4 : 4 + EXPERTS], refs[4 + EXPERTS + earlier :]
    tokens = streams[0].shape[0]
    for i in range(2):
        weights = combines[i][...]
        high = weights.astype(jnp.bfloat16)
        left = weights - high.astype(jnp.float32)
        middle = left.astype(jnp.bfloat16)
        low = (left - middle.astype(jnp.float32)).astype(jnp.bfloat16)
        terms = jnp.concatenate([high, middle, low], axis=0)
        rows = jnp.concatenate([block[i * SLOTS : (i + 1) * SLOTS] for block in blocks], axis=0)
        sums = mm(terms, rows)
        mixture = sums[:tokens] + sums[tokens : 2 * tokens] + sums[2 * tokens :]
        outs[i][...] = (streams[i][...].astype(jnp.float32) + mixture).astype(jnp.bfloat16)


def finish(streams, combines, blocks, side, begun):
    tokens, width = streams[0].shape
    deep = width // 4
    steps = blocks[0].shape[1] // deep
    column = pl.BlockSpec((tokens, deep), lambda k: (0, steps * side + k))
    return pl.pallas_call(
        functools.partial(finish_kernel, len(begun)),
        grid=(steps,),
        out_shape=[jax.ShapeDtypeStruct((tokens, width), jnp.bfloat16)] * 2,
        in_specs=[column] * 2
        + [pl.BlockSpec((tokens, GROUP), lambda k: (0, 0))] * 2
        + [pl.BlockSpec((2 * SLOTS, deep), lambda k: (0, k))] * EXPERTS
        + [ANY] * len(begun),
        out_specs=[column] * 2,
        input_output_aliases={4 + EXPERTS + i: i for i in range(len(begun))},
        compiler_params=pltpu.CompilerParams(vmem_limit_bytes=ROOM),
        cost_estimate=pl.CostEstimate(flops=6 * GROUP * width * tokens, bytes_accessed=8 * tokens * width, transcendentals=0),
        name="finish",
    )(*streams, *combines, *blocks, *begun)


def after(value, earlier):
    return pl.pallas_call(
        lambda *refs: None,
        out_shape=jax.ShapeDtypeStruct(value.shape, value.dtype),
        in_specs=[ANY] * (1 + len(earlier)),
        out_specs=ANY,
        input_output_aliases={0: 0},
        cost_estimate=pl.CostEstimate(flops=0, bytes_accessed=0, transcendentals=0),
        name="after",
    )(value, *earlier)


def exchange(blocks, sign, order, depth):
    out = {0: blocks[0]}
    for k, i in enumerate(order):
        block = after(blocks[i], (out[order[k - depth]],)) if k >= depth else blocks[i]
        out[i] = moved(block, sign * BLOCKS[i][0], BLOCKS[i][1])
    return [out[i] for i in range(EXPERTS)]


def body(up_prev, down_prev, enter_up, enter_down, norm_gain, router, w_gate, w_up, w_down, ids_up, ids_down):
    from_below = from_behind(up_prev[0], "pipe", 1)
    from_above = from_behind(down_prev[0], "pipe", -1)

    def of_core(value):
        return moved(value, 0, 0, 1)

    def of_pair(value):
        return moved(value, 0, 1)

    gate, up, whole = w_gate[0], w_up[0], w_down[0]
    gate_core, up_core = of_core(gate), of_core(up)
    blocks, streams, combines = prepare(
        from_below, from_above, enter_up, enter_down, norm_gain, router[0].T, ids_up[0], ids_down[0], (gate_core, up_core)
    )
    gate_pair, up_pair = of_pair(gate), of_pair(up)
    rows = exchange(blocks, 1, ORDER, 3)
    half = whole.shape[1] // 2
    low_pair = of_pair(after(whole[:, :half], (rows[ORDER[2]],)))
    high_pair = of_pair(after(whole[:, half:], (rows[ORDER[5]],)))
    gate_pair, up_pair = after(gate_pair, rows[1:]), after(up_pair, rows[1:])
    units = hidden(rows, (gate, gate_core, gate_pair, of_core(gate_pair)), (up, up_core, up_pair, of_core(up_pair)))
    own = (whole, of_core(whole))
    low_pair = after(low_pair, (units,))
    back = exchange(down(units, own, (low_pair, of_core(low_pair)), 0), -1, ORDER_LOW, 5)
    high_pair = after(high_pair, [back[i] for i in ORDER_LOW[:4]])
    outs = finish(streams, combines, back, 0, ())
    back = exchange(down(units, own, (high_pair, of_core(high_pair)), 1), -1, ORDER_HIGH, 5)
    outs = finish(streams, combines, back, 1, outs)
    return outs[0][None], outs[1][None]


def solution(mesh):
    in_specs = (
        P("pipe", "expert", None),
        P("pipe", "expert", None),
        P("expert", None),
        P("expert", None),
        P("pipe", None),
        P("pipe", None, None),
        P("pipe", None, "expert"),
        P("pipe", None, "expert"),
        P("pipe", "expert", None),
        P("pipe", "expert", None),
        P("pipe", "expert", None),
    )
    out_specs = (P("pipe", "expert", None), P("pipe", "expert", None))
    return jax.shard_map(body, mesh=mesh, in_specs=in_specs, out_specs=out_specs, check_vma=False)
```

```python
import functools

import jax
import jax.numpy as jnp
from jax import lax
from jax.experimental import pallas as pl
from jax.experimental.pallas import tpu as pltpu
from jax.sharding import PartitionSpec as P

EXPERTS = 8
SLOTS = 32
SIDE = 4
GROUP = EXPERTS * SLOTS
CHUNK = 512
ROOM = 60 * 1024 * 1024
VMEM = pl.BlockSpec(memory_space=pltpu.VMEM)
ANY = pl.BlockSpec(memory_space=pl.ANY)


def place(x, y, core):
    return (x * SIDE + y) * 2 + core


def moved(value, by_x, xor_y, xor_core=0):
    pairs = [
        (place(x, y, c), place((x + by_x) % SIDE, y ^ xor_y, c ^ xor_core))
        for x in range(SIDE)
        for y in range(SIDE)
        for c in range(2)
    ]
    return lax.ppermute(value, "expert", pairs)


BLOCKS = [(by_x, xor_y) for xor_y in (0, 3) for by_x in range(SIDE)]
ORDER = [5, 7, 2, 4, 1, 3, 6]
ORDER_LOW = [5, 7, 2, 4, 1, 3, 6]
ORDER_HIGH = [6, 2, 5, 7, 1, 3, 4]


def from_behind(value, axis, by):
    devices = lax.axis_size(axis)
    pairs = [(i, i + by) for i in range(devices) if 0 <= i + by < devices]
    return lax.ppermute(value, axis, pairs)


def mm(a, b, dims=((1,), (0,))):
    return lax.dot_general(a, b, (dims, ((), ())), preferred_element_type=jnp.float32)


def chunks_of(width):
    return [slice(at, min(at + CHUNK, width)) for at in range(0, width, CHUNK)]


def prepare_one(at_end, at_row, recv, enter, gain, router_t, ids, blocks, stream, combine, normed):
    tokens, width = recv.shape
    edge = lax.axis_index("pipe") == (lax.axis_size("pipe") - 1 if at_end else 0)
    total = jnp.zeros((tokens, 1), jnp.float32)
    for cut in chunks_of(width):
        values = jnp.where(edge, enter[:, cut].astype(jnp.float32), recv[:, cut].astype(jnp.float32))
        stream[:, cut] = values.astype(jnp.bfloat16)
        total += jnp.sum(values * values, axis=-1, keepdims=True)
    scale = lax.rsqrt(total / width + 1e-06)
    logits = jnp.zeros((EXPERTS, tokens), jnp.float32)
    for cut in chunks_of(width):
        part = (stream[:, cut].astype(jnp.float32) * scale * gain[:, cut]).astype(jnp.bfloat16)
        normed[:, cut] = part
        logits += mm(router_t[:, cut], part, ((1,), (1,)))

    row = lax.broadcasted_iota(jnp.int32, (tokens, tokens), 0)
    col = lax.broadcasted_iota(jnp.int32, (tokens, tokens), 1)
    expert = lax.broadcasted_iota(jnp.int32, (EXPERTS, tokens), 0)
    picks = [ids[k : k + 1, :] == expert for k in range(2)]
    marks = jnp.where(picks[0] | picks[1], 1.0, 0.0).astype(jnp.bfloat16)
    spot = lax.axis_index("expert")
    my_x, my_half = lax.div(spot, 2 * SIDE), lax.rem(lax.div(spot, 4), 2)
    step = lax.rem(lax.div(expert, 2) - my_x + SIDE, SIDE)
    block = (lax.rem(expert, 2) ^ my_half) * SIDE + step
    at = (block * SLOTS).astype(jnp.float32) + mm(marks, jnp.where(row < col, 1.0, 0.0).astype(jnp.bfloat16))
    affinity = [jax.nn.sigmoid(jnp.sum(jnp.where(pick, logits, 0.0), axis=0, keepdims=True)) for pick in picks]
    both = affinity[0] + affinity[1]
    slot = lax.broadcasted_iota(jnp.int32, (GROUP, tokens), 0)
    placing = jnp.zeros((GROUP, tokens), jnp.float32)
    weighted = jnp.zeros((GROUP, tokens), jnp.float32)
    for pick, share in zip(picks, affinity):
        where = jnp.sum(jnp.where(pick, at, 0.0), axis=0, keepdims=True).astype(jnp.int32)
        placing += jnp.where(slot == where, 1.0, 0.0)
        weighted += jnp.where(slot == where, 2.5 * share / both, 0.0)
    placing = placing.astype(jnp.bfloat16)
    for cut in chunks_of(width):
        rows = mm(placing, normed[:, cut]).astype(jnp.bfloat16)
        for i, out in enumerate(blocks):
            out[at_row : at_row + SLOTS, cut] = rows[i * SLOTS : (i + 1) * SLOTS]
    padded = jnp.concatenate([weighted, jnp.zeros((GROUP, -tokens % 128), jnp.float32)], axis=1)
    combine[...] = padded.T[:tokens]


def prepare_kernel(earlier, recv_up, recv_down, enter_up, enter_down, gain, router_t, ids_up, ids_down, *rest):
    rest = rest[earlier:]
    blocks, (stream_up, stream_down, combine_up, combine_down, normed) = rest[:EXPERTS], rest[EXPERTS:]
    prepare_one(False, 0, recv_up, enter_up, gain, router_t, ids_up, blocks, stream_up, combine_up, normed)
    prepare_one(True, SLOTS, recv_down, enter_down, gain, router_t, ids_down, blocks, stream_down, combine_down, normed)


def prepare(recv_up, recv_down, enter_up, enter_down, gain, router_t, ids_up, ids_down, earlier):
    tokens, width = recv_up.shape
    shape = jax.ShapeDtypeStruct
    out = pl.pallas_call(
        functools.partial(prepare_kernel, len(earlier)),
        out_shape=[shape((2 * SLOTS, width), jnp.bfloat16)] * EXPERTS
        + [shape((tokens, width), jnp.bfloat16)] * 2
        + [shape((tokens, GROUP), jnp.float32)] * 2,
        in_specs=[VMEM] * 8 + [ANY] * len(earlier),
        out_specs=[VMEM] * (EXPERTS + 4),
        scratch_shapes=[pltpu.VMEM((tokens, width), jnp.bfloat16)],
        compiler_params=pltpu.CompilerParams(vmem_limit_bytes=ROOM),
        cost_estimate=pl.CostEstimate(flops=4 * GROUP * tokens * width, bytes_accessed=24 * tokens * width, transcendentals=0),
        name="prepare",
    )(recv_up, recv_down, enter_up, enter_down, gain, router_t, ids_up.T, ids_down.T, *earlier)
    return out[:EXPERTS], out[EXPERTS : EXPERTS + 2], out[EXPERTS + 2 :]


def hidden_kernel(*refs):
    blocks, gates, ups = refs[:EXPERTS], refs[EXPERTS : EXPERTS + 4], refs[EXPERTS + 4 : EXPERTS + 8]
    units, gate_sum, up_sum = refs[EXPERTS + 8 :]
    step = pl.program_id(0)

    @pl.when(step == 0)
    def _():
        gate_sum[...] = jnp.zeros_like(gate_sum)
        up_sum[...] = jnp.zeros_like(up_sum)

    rows = jnp.concatenate([block[...] for block in blocks], axis=0)
    part = gates[0].shape[1]
    for total, mats in ((gate_sum, gates), (up_sum, ups)):
        for i, mat in enumerate(mats):
            total[:, i * part : (i + 1) * part] += mm(rows, mat[...])

    @pl.when(step == pl.num_programs(0) - 1)
    def _():
        units[...] = (jax.nn.silu(gate_sum[...]) * up_sum[...]).astype(jnp.bfloat16)


def hidden(blocks, gates, ups):
    width, part = gates[0].shape
    deep = width // 2
    rows = 2 * GROUP
    return pl.pallas_call(
        hidden_kernel,
        grid=(width // deep,),
        out_shape=jax.ShapeDtypeStruct((rows, 4 * part), jnp.bfloat16),
        in_specs=[pl.BlockSpec((2 * SLOTS, deep), lambda k: (0, k))] * EXPERTS
        + [pl.BlockSpec((deep, part), lambda k: (k, 0))] * 8,
        out_specs=pl.BlockSpec((rows, 4 * part), lambda k: (0, 0)),
        scratch_shapes=[pltpu.VMEM((rows, 4 * part), jnp.float32)] * 2,
        compiler_params=pltpu.CompilerParams(vmem_limit_bytes=ROOM),
        cost_estimate=pl.CostEstimate(flops=0, bytes_accessed=0, transcendentals=0),
        name="hidden",
    )(*blocks, *gates, *ups)


def down_kernel(units, mat_a, mat_b, mat_c, mat_d, *blocks):
    mat = jnp.concatenate([mat_a[...], mat_b[...], mat_c[...], mat_d[...]], axis=0)
    rows = mm(units[...], mat).astype(jnp.bfloat16)
    for i, out in enumerate(blocks):
        out[...] = rows[i * 2 * SLOTS : (i + 1) * 2 * SLOTS]


def down(units, whole, parts, side):
    part, width = parts[0].shape
    deep = width // 2
    return pl.pallas_call(
        down_kernel,
        grid=(2,),
        out_shape=[jax.ShapeDtypeStruct((2 * SLOTS, width), jnp.bfloat16)] * EXPERTS,
        in_specs=[pl.BlockSpec(units.shape, lambda k: (0, 0))]
        + [pl.BlockSpec((part, deep), lambda k: (0, 2 * side + k))] * 2
        + [pl.BlockSpec((part, deep), lambda k: (0, k))] * 2,
        out_specs=[pl.BlockSpec((2 * SLOTS, deep), lambda k: (0, k))] * EXPERTS,
        compiler_params=pltpu.CompilerParams(vmem_limit_bytes=ROOM),
        cost_estimate=pl.CostEstimate(flops=0, bytes_accessed=0, transcendentals=0),
        name="down",
    )(units, *whole, *parts)


def finish_kernel(earlier, *refs):
    streams, combines, blocks, outs = refs[:2], refs[2:4], refs[4 : 4 + EXPERTS], refs[4 + EXPERTS + earlier :]
    tokens = streams[0].shape[0]
    for i in range(2):
        weights = combines[i][...]
        high = weights.astype(jnp.bfloat16)
        left = weights - high.astype(jnp.float32)
        middle = left.astype(jnp.bfloat16)
        low = (left - middle.astype(jnp.float32)).astype(jnp.bfloat16)
        terms = jnp.concatenate([high, middle, low], axis=0)
        rows = jnp.concatenate([block[i * SLOTS : (i + 1) * SLOTS] for block in blocks], axis=0)
        sums = mm(terms, rows)
        mixture = sums[:tokens] + sums[tokens : 2 * tokens] + sums[2 * tokens :]
        outs[i][...] = (streams[i][...].astype(jnp.float32) + mixture).astype(jnp.bfloat16)


def finish(streams, combines, blocks, side, begun):
    tokens, width = streams[0].shape
    deep = width // 4
    steps = blocks[0].shape[1] // deep
    column = pl.BlockSpec((tokens, deep), lambda k: (0, steps * side + k))
    return pl.pallas_call(
        functools.partial(finish_kernel, len(begun)),
        grid=(steps,),
        out_shape=[jax.ShapeDtypeStruct((tokens, width), jnp.bfloat16)] * 2,
        in_specs=[column] * 2
        + [pl.BlockSpec((tokens, GROUP), lambda k: (0, 0))] * 2
        + [pl.BlockSpec((2 * SLOTS, deep), lambda k: (0, k))] * EXPERTS
        + [ANY] * len(begun),
        out_specs=[column] * 2,
        input_output_aliases={4 + EXPERTS + i: i for i in range(len(begun))},
        compiler_params=pltpu.CompilerParams(vmem_limit_bytes=ROOM),
        cost_estimate=pl.CostEstimate(flops=6 * GROUP * width * tokens, bytes_accessed=8 * tokens * width, transcendentals=0),
        name="finish",
    )(*streams, *combines, *blocks, *begun)


def after(value, earlier):
    return pl.pallas_call(
        lambda *refs: None,
        out_shape=jax.ShapeDtypeStruct(value.shape, value.dtype),
        in_specs=[ANY] * (1 + len(earlier)),
        out_specs=ANY,
        input_output_aliases={0: 0},
        cost_estimate=pl.CostEstimate(flops=0, bytes_accessed=0, transcendentals=0),
        name="after",
    )(value, *earlier)


def exchange(blocks, sign, order, depth):
    out = {0: blocks[0]}
    for k, i in enumerate(order):
        block = after(blocks[i], (out[order[k - depth]],)) if k >= depth else blocks[i]
        out[i] = moved(block, sign * BLOCKS[i][0], BLOCKS[i][1])
    return [out[i] for i in range(EXPERTS)]


def body(up_prev, down_prev, enter_up, enter_down, norm_gain, router, w_gate, w_up, w_down, ids_up, ids_down):
    from_below = from_behind(up_prev[0], "pipe", 1)
    from_above = from_behind(down_prev[0], "pipe", -1)

    def of_core(value):
        return moved(value, 0, 0, 1)

    def of_pair(value):
        return moved(value, 0, 1)

    gate, up, whole = w_gate[0], w_up[0], w_down[0]
    gate_core, up_core = of_core(gate), of_core(up)
    blocks, streams, combines = prepare(
        from_below, from_above, enter_up, enter_down, norm_gain, router[0].T, ids_up[0], ids_down[0], (gate_core, up_core)
    )
    gate_pair, up_pair = of_pair(gate), of_pair(up)
    rows = exchange(blocks, 1, ORDER, 3)
    half = whole.shape[1] // 2
    low_pair = of_pair(after(whole[:, :half], (rows[ORDER[2]],)))
    high_pair = of_pair(after(whole[:, half:], (rows[ORDER[5]],)))
    gate_pair, up_pair = after(gate_pair, rows[1:]), after(up_pair, rows[1:])
    units = hidden(rows, (gate, gate_core, gate_pair, of_core(gate_pair)), (up, up_core, up_pair, of_core(up_pair)))
    own = (whole, of_core(whole))
    low_pair = after(low_pair, (units,))
    back = exchange(down(units, own, (low_pair, of_core(low_pair)), 0), -1, ORDER_LOW, 5)
    high_pair = after(high_pair, [back[i] for i in ORDER_LOW[:4]])
    outs = finish(streams, combines, back, 0, ())
    back = exchange(down(units, own, (high_pair, of_core(high_pair)), 1), -1, ORDER_HIGH, 5)
    outs = finish(streams, combines, back, 1, outs)
    return outs[0][None], outs[1][None]


def solution(mesh):
    in_specs = (
        P("pipe", "expert", None),
        P("pipe", "expert", None),
        P("expert", None),
        P("expert", None),
        P("pipe", None),
        P("pipe", None, None),
        P("pipe", None, "expert"),
        P("pipe", None, "expert"),
        P("pipe", "expert", None),
        P("pipe", "expert", None),
        P("pipe", "expert", None),
    )
    out_specs = (P("pipe", "expert", None), P("pipe", "expert", None))
    return jax.shard_map(body, mesh=mesh, in_specs=in_specs, out_specs=out_specs, check_vma=False)
```
